32 devices in a mesh: row: 8 (over y, x, core), col: 4 (over z).
Axes of the slice: x: 2, y: 2, z: 4, core: 2. Of those that a mesh axis runs over, the one named last changes fastest.
Arguments:
- amplitudes: bfloat16 [64, 6400], P(('col', 'row')), may hold values from -6 to 6
- panel: bfloat16 [9600, 6400], P('col', 'row'), may hold values from -0.21875 to 0.21875
- irrep_ij: int32 [64], replicated, may hold values from 0 to 7
- irrep_ef: int32 [6400], replicated, may hold values from 0 to 7
Outputs:
- ladder: bfloat16 [64, 9600], P(('col', 'row'))
The draws below stay inside these ranges and needn't reach their ends.
All inputs are finite; a program needn't handle non-finite values.
Results may differ from the reference program's by a relative error of at most 0.003.
Values may be sent and summed in bfloat16 or wider, within the bound.
A program may use at most 64 MiB of HBM per device.

```python
import jax
import jax.numpy as jnp
from jax import lax

EF = 6400
AB = 9600
IJ = 64


def place_ends(entries, rng, least, high):
    shape = entries.shape
    index_at = [jax.random.randint(jax.random.fold_in(rng, axis), (), 0, shape[axis]) for axis in range(len(shape))]
    entries = entries.at[tuple(index_at)].set(least)
    longest = shape.index(max(shape))
    index_at[longest] = (index_at[longest] + 1) % shape[longest]
    return entries.at[tuple(index_at)].set(high)


def spiked(values, rng, source, target, parts, factor):
    def block_of(position):
        return (jnp.arange(values.shape[position]) // (values.shape[position] // parts)).reshape((-1,) + (1,) * (values.ndim - 1 - position))

    one_side = jax.random.permutation(rng, parts)[block_of(target)]
    second = (block_of(target) + parts // 2) % parts
    return jnp.where((block_of(source) == one_side) | (block_of(source) == second), factor * values, values)


def block_levels(rng, dims, shards, smallest, top_value):
    level = 1.0
    for dim, blocks in shards:
        draws = jax.random.uniform(jax.random.fold_in(jax.random.fold_in(rng, 6), dim), (blocks,), jnp.float32, smallest / len(shards), top_value / len(shards))
        level = level * jnp.repeat(jnp.exp(draws), dims[dim] // blocks).reshape((-1,) + (1,) * (len(dims) - 1 - dim))
    return level


def scatter_about(stream_key, extent, spread, reach, shards=(), held_as=jnp.bfloat16):
    drawn = spread * jax.random.normal(stream_key, extent, jnp.float32)
    if shards:
        drawn = drawn * block_levels(stream_key, extent, shards, -0.22, 0.18)
    return jnp.clip(drawn, -reach, reach).astype(held_as)


def gaussian_with(rng, dims, deviation, most, split, heavy, held_as=jnp.bfloat16):
    array = deviation * jax.random.normal(rng, dims, jnp.float32)
    if split:
        array = array * block_levels(rng, dims, split, -0.22, 0.18)
    return jnp.clip(spiked(array, jax.random.fold_in(rng, 3), *heavy), -most, most).astype(held_as)


def setup_inputs(seed: int = 0) -> dict:
    key_of = jax.random.split(jax.random.key(seed), 5)
    amplitudes = gaussian_with(key_of[0], (IJ, EF), 1.0, 6.0, ((0, 32),), (1, 0, 32, 2.75))
    panel = scatter_about(key_of[1], (AB, EF), (EF // 8) ** -0.5, 0.21875, ((0, 4), (1, 8)))
    irrep_ij = place_ends(jax.random.randint(key_of[2], (IJ,), 0, 8), jax.random.fold_in(key_of[2], 1), 0, 7).astype(jnp.int32)
    irrep_ef = place_ends(jax.random.randint(key_of[3], (EF,), 0, 8), jax.random.fold_in(key_of[3], 1), 0, 7).astype(jnp.int32)
    return dict(amplitudes=amplitudes, panel=panel, irrep_ij=irrep_ij, irrep_ef=irrep_ef)


def reference(amplitudes, panel, irrep_ij, irrep_ef):
    same = irrep_ij[:, None] == irrep_ef[None, :]
    allowed = jnp.where(same, amplitudes, jnp.zeros_like(amplitudes))
    total = lax.dot_general(allowed, panel, (((1,), (1,)), ((), ())), preferred_element_type=jnp.float32)
    return total.astype(jnp.bfloat16)
```

```python
import functools

import jax
import jax.numpy as jnp
from jax import lax
from jax.experimental import pallas as pl
from jax.experimental.pallas import tpu as pltpu
from jax.sharding import PartitionSpec as P

TILE = 512


def tiles(ab):
    return [(at, min(TILE, ab - at)) for at in range(0, ab, TILE)]


def remote(src, dst, send_sem, recv_sem, **device):
    return pltpu.make_async_remote_copy(
        src_ref=src, dst_ref=dst, send_sem=send_sem, recv_sem=recv_sem,
        device_id=device, device_id_type=pl.DeviceIdType.MESH,
    )


def kernel(R, C, amp_ref, sym_ij_ref, sym_ef_ref, panel_ref, out_ref,
           panel_v, slabs, met, rows16, gathered, allowed, part, from_pair, summed, from_chips, outgoing, landed,
           panel_sem, s1, r1, s2, r2, s3, r3, s4, r4, s5, r5):
    r = lax.axis_index("row")
    c = lax.axis_index("col")
    k = lax.rem(r, 2)
    q = r // 2
    Q = R // 2
    J, EF = amp_ref.shape
    ef = EF // R
    ab = panel_v.shape[1]

    load = pltpu.make_async_copy(panel_ref, panel_v, panel_sem)
    load.start()

    barrier = pltpu.get_barrier_semaphore()
    for d in range(1, R):
        pl.semaphore_signal(barrier, inc=1, device_id={"row": lax.rem(r + d, R)}, device_id_type=pl.DeviceIdType.MESH)
    for d in range(1, C):
        pl.semaphore_signal(barrier, inc=1, device_id={"col": lax.rem(c + d, C)}, device_id_type=pl.DeviceIdType.MESH)

    first = (c * R + r) * J
    sym_ef = sym_ef_ref[...].reshape(1, EF)
    which = lax.broadcasted_iota(jnp.int32, (J, EF), 0)
    sym_ij = jnp.full((J, EF), sym_ij_ref[first], jnp.int32)
    for j in range(1, J):
        sym_ij = jnp.where(which == j, sym_ij_ref[first + j], sym_ij)
    masked = jnp.where(sym_ij == sym_ef, amp_ref[...].astype(jnp.float32), 0.0)
    for p in range(R):
        slabs[p] = masked[:, p * ef:(p + 1) * ef]

    pl.semaphore_wait(barrier, R + C - 2)

    sends = []
    for d in range(1, R):
        to = lax.rem(r + d, R)
        send = remote(slabs.at[to], met.at[r], s1.at[d], r1.at[d], row=to)
        send.start()
        sends.append(send)
    met[r] = slabs[r]
    for send in sends:
        send.wait_recv()
    for p in range(R):
        rows16[pl.ds(p * J, J), :] = met[p]
    gathered[c] = rows16[...].astype(jnp.bfloat16)

    more = []
    for d in range(1, C):
        to = lax.rem(c + d, C)
        send = remote(gathered.at[c], gathered.at[c], s2.at[d], r2.at[d], col=to)
        send.start()
        more.append(send)

    total_rows = R * C * J
    group = next(g for g in (8, 4, 2, 1) if Q % min(g, Q) == 0 and min(g, Q) * C * J <= 256)
    group = min(group, Q)
    picks = []
    for half in range(2):
        for start in range(0, Q, group):
            blocks = []
            for p in range(start, start + group):
                at = lax.broadcasted_iota(jnp.int32, (C * J, total_rows), 0)
                source = (at // J) * (R * J) + (2 * p + half) * J + lax.rem(at, J)
                blocks.append(source == lax.broadcasted_iota(jnp.int32, (C * J, total_rows), 1))
            picks.append((half, start, blocks))

    for send in more:
        send.wait_recv()
    everything = gathered[...].reshape(total_rows, ef)
    for half, start, blocks in picks:
        pick = jnp.concatenate([jnp.where(b, 1.0, 0.0) for b in blocks], axis=0).astype(jnp.bfloat16)
        allowed[half, pl.ds(start * C * J, group * C * J), :] = jnp.dot(
            pick, everything, preferred_element_type=jnp.float32
        ).astype(jnp.bfloat16)

    def multiply(half):
        left = allowed[half]
        for at, size in tiles(ab):
            part[half, :, pl.ds(at, size)] = lax.dot_general(
                left, panel_v[:, pl.ds(at, size)], (((1,), (0,)), ((), ())), preferred_element_type=jnp.float32
            )

    load.wait()
    multiply(1 - k)
    pair = remote(part.at[1 - k], from_pair, s3, r3, row=2 * q + 1 - k)
    pair.start()
    multiply(k)
    pair.wait_recv()

    for p in range(Q):
        at = pl.ds(p * C * J, C * J)
        summed[p] = part[k, at, :] + from_pair[at, :]
    chips = []
    for d in range(1, Q):
        to = lax.rem(q + d, Q)
        send = remote(summed.at[to], from_chips.at[d - 1], s4.at[d], r4.at[d], row=2 * to + k)
        send.start()
        chips.append(send)
    total = summed[q]
    for d, send in enumerate(chips):
        send.wait_recv()
        total = total + from_chips[d]
    for p in range(C):
        outgoing[p] = total[p * J:(p + 1) * J, :]
    last = []
    for d in range(1, C):
        to = lax.rem(c + d, C)
        send = remote(outgoing.at[to], landed.at[c], s5.at[d], r5.at[d], col=to)
        send.start()
        last.append(send)
    landed[c] = outgoing[c]
    for send in last:
        send.wait_recv()
    for p in range(C):
        out_ref[:, p * ab:(p + 1) * ab] = landed[p].astype(jnp.bfloat16)
    pair.wait_send()
    for send in sends + more + chips + last:
        send.wait_send()


def solution(mesh):
    R, C = mesh.shape["row"], mesh.shape["col"]

    def body(amplitudes, panel, irrep_ij, irrep_ef):
        J, EF = amplitudes.shape
        ab, ef = panel.shape
        Q = R // 2
        H = Q * C * J
        f32, bf16 = jnp.float32, jnp.bfloat16
        dma = pltpu.SemaphoreType.DMA
        return pl.pallas_call(
            functools.partial(kernel, R, C),
            out_shape=jax.ShapeDtypeStruct((J, C * ab), bf16),
            in_specs=[
                pl.BlockSpec(memory_space=pltpu.VMEM),
                pl.BlockSpec(memory_space=pltpu.SMEM),
                pl.BlockSpec(memory_space=pltpu.VMEM),
                pl.BlockSpec(memory_space=pl.ANY),
            ],
            out_specs=pl.BlockSpec(memory_space=pltpu.VMEM),
            scratch_shapes=[
                pltpu.VMEM((ef, ab), bf16),
                pltpu.VMEM((R, J, ef), f32),
                pltpu.VMEM((R, J, ef), f32),
                pltpu.VMEM((R * J, ef), f32),
                pltpu.VMEM((C, R * J, ef), bf16),
                pltpu.VMEM((2, H, ef), bf16),
                pltpu.VMEM((2, H, ab), f32),
                pltpu.VMEM((H, ab), f32),
                pltpu.VMEM((Q, C * J, ab), f32),
                pltpu.VMEM((max(Q - 1, 1), C * J, ab), f32),
                pltpu.VMEM((C, J, ab), f32),
                pltpu.VMEM((C, J, ab), f32),
                dma,
                dma((R,)), dma((R,)),
                dma((C,)), dma((C,)),
                dma, dma,
                dma((Q,)), dma((Q,)),
                dma((C,)), dma((C,)),
            ],
            compiler_params=pltpu.CompilerParams(
                collective_id=0, has_side_effects=True, vmem_limit_bytes=60 << 20
            ),
            cost_estimate=pl.CostEstimate(
                flops=2 * R * C * J * ef * ab, bytes_accessed=2 * ab * ef, transcendentals=0
            ),
        )(amplitudes, irrep_ij, irrep_ef, panel.T)

    in_specs = (P(("col", "row"), None), P("col", "row"), P(), P())
    return jax.shard_map(body, mesh=mesh, in_specs=in_specs, out_specs=P(("col", "row"), None), check_vma=False)
```

```python
import functools

import jax
import jax.numpy as jnp
from jax import lax
from jax.experimental import pallas as pl
from jax.experimental.pallas import tpu as pltpu
from jax.sharding import PartitionSpec as P

CHUNKS = 3


def chunks(ab, n):
    step = ab // n // 128 * 128
    return [(j * step, step if j < n - 1 else ab - j * step) for j in range(n)]


def remote(src, dst, send_sem, recv_sem, **device):
    return pltpu.make_async_remote_copy(
        src_ref=src, dst_ref=dst, send_sem=send_sem, recv_sem=recv_sem,
        device_id=device, device_id_type=pl.DeviceIdType.MESH,
    )


def direct(R, C, N, amp_ref, sym_ij_ref, sym_ef_ref, panel_ref, out_ref,
           panel_v, wide, slabs, pick, gathered, allowed, part, from_pair, summed, from_chips, outgoing, landed,
           panel_sem, s1, r1, s3, r3, s4, r4, s5, r5):
    r = lax.axis_index("row")
    c = lax.axis_index("col")
    k = lax.rem(r, 2)
    q = r // 2
    Q = R // 2
    J, EF = amp_ref.shape
    ef = EF // R
    ab = panel_v.shape[1]

    load = pltpu.make_async_copy(panel_ref, panel_v, panel_sem)
    load.start()

    lanes = [(at, min(128, ef - at)) for at in range(0, ef, 128)]
    L = 8
    D = R * C
    peers = [(dr, dc) for dc in reversed(range(C)) for dr in reversed(range(R)) if (dr, dc) != (0, 0)]

    barrier = pltpu.get_barrier_semaphore()
    for dr, dc in peers:
        pl.semaphore_signal(
            barrier, inc=1, device_id={"row": lax.rem(r + dr, R), "col": lax.rem(c + dc, C)},
            device_id_type=pl.DeviceIdType.MESH,
        )

    first = (c * R + r) * J
    sym_ef = sym_ef_ref[...].reshape(1, EF)
    which = lax.broadcasted_iota(jnp.int32, (J, EF), 0)
    sym_ij = jnp.full((J, EF), sym_ij_ref[first], jnp.int32)
    for j in range(1, J):
        sym_ij = jnp.where(which == j, sym_ij_ref[first + j], sym_ij)
    masked = jnp.where(sym_ij == sym_ef, amp_ref[...].astype(jnp.float32), 0.0)
    wide[...] = jnp.zeros_like(wide)
    for p in range(R):
        for i, (at, size) in enumerate(lanes):
            for j in range(J):
                wide[p, j * L + i:j * L + i + 1, 0:size] = masked[j:j + 1, p * ef + at:p * ef + at + size]
    slabs[...] = wide[...].astype(jnp.bfloat16)

    at = lax.broadcasted_iota(jnp.int32, (C * J, D * J * L), 0)
    held = lax.broadcasted_iota(jnp.int32, (C * J, D * J * L), 1)
    base = (at // J) * (R * J * L) + lax.rem(at, J) * L
    for half in range(2):
        for p in range(Q):
            for i in range(len(lanes)):
                pick[i, half, pl.ds(p * C * J, C * J), :] = jnp.where(
                    base + ((2 * p + half) * J * L + i) == held, 1.0, 0.0)
    picks = pick[...].reshape(len(lanes) * D * J, D * J * L).astype(jnp.bfloat16)

    pl.semaphore_wait(barrier, D - 1)

    sends = []
    for dr, dc in peers:
        row, col = lax.rem(r + dr, R), lax.rem(c + dc, C)
        send = remote(slabs.at[row], gathered.at[c * R + r], s1.at[dc * R + dr], r1.at[dc * R + dr], row=row, col=col)
        send.start()
        sends.append(send)
    gathered[c * R + r] = slabs[r]
    for send in sends:
        send.wait_recv()
    picked = jnp.dot(picks, gathered[...].reshape(D * J * L, 128), preferred_element_type=jnp.float32)
    for i, (at, size) in enumerate(lanes):
        for half in range(2):
            start = (i * 2 + half) * Q * C * J
            allowed[half, :, at:at + size] = picked[start:start + Q * C * J, :size].astype(jnp.bfloat16)

    cuts = chunks(ab, N)

    def multiply(half, j):
        at, size = cuts[j]
        part[j][half] = jnp.dot(allowed[half], panel_v[:, pl.ds(at, size)], preferred_element_type=jnp.float32)

    load.wait()
    pairs, chips, last = [], [], []

    def reduce_pair(j):
        pairs[j].wait_recv()
        for p in range(Q):
            at = pl.ds(p * C * J, C * J)
            summed[j][p] = part[j][k, at, :] + from_pair[j][at, :]
        chips.append([])
        for d in range(1, Q):
            to = lax.rem(q + d, Q)
            send = remote(summed[j].at[to], from_chips[j].at[d - 1], s4.at[j, d], r4.at[j, d], row=2 * to + k)
            send.start()
            chips[j].append(send)

    for j in range(len(cuts)):
        multiply(1 - k, j)
        pair = remote(part[j].at[1 - k], from_pair[j], s3.at[j], r3.at[j], row=2 * q + 1 - k)
        pair.start()
        pairs.append(pair)
        multiply(k, j)
        if j > 0:
            reduce_pair(j - 1)
    reduce_pair(len(cuts) - 1)

    for j in range(len(cuts)):
        total = summed[j][q]
        for d, send in enumerate(chips[j]):
            send.wait_recv()
            total = total + from_chips[j][d]
        for p in range(C):
            outgoing[j][p] = total[p * J:(p + 1) * J, :]
        last.append([])
        for d in range(1, C):
            to = lax.rem(c + d, C)
            send = remote(outgoing[j].at[to], landed[j].at[c], s5.at[j, d], r5.at[j, d], col=to)
            send.start()
            last[j].append(send)
        landed[j][c] = outgoing[j][c]
    for j, (at, size) in enumerate(cuts):
        for send in last[j]:
            send.wait_recv()
        for p in range(C):
            out_ref[:, p * ab + at:p * ab + at + size] = landed[j][p].astype(jnp.bfloat16)
    for send in sends + pairs + sum(chips, []) + sum(last, []):
        send.wait_send()


def staged(R, C, N, amp_ref, sym_ij_ref, sym_ef_ref, panel_ref, out_ref,
           panel_v, slabs, met, rows16, gathered, allowed, part, from_pair, summed, from_chips, outgoing, landed,
           panel_sem, s1, r1, s2, r2, s3, r3, s4, r4, s5, r5):
    r = lax.axis_index("row")
    c = lax.axis_index("col")
    k = lax.rem(r, 2)
    q = r // 2
    Q = R // 2
    J, EF = amp_ref.shape
    ef = EF // R
    ab = panel_v.shape[1]

    load = pltpu.make_async_copy(panel_ref, panel_v, panel_sem)
    load.start()

    barrier = pltpu.get_barrier_semaphore()
    for d in range(1, R):
        pl.semaphore_signal(barrier, inc=1, device_id={"row": lax.rem(r + d, R)}, device_id_type=pl.DeviceIdType.MESH)
    for d in range(1, C):
        pl.semaphore_signal(barrier, inc=1, device_id={"col": lax.rem(c + d, C)}, device_id_type=pl.DeviceIdType.MESH)

    first = (c * R + r) * J
    sym_ef = sym_ef_ref[...].reshape(1, EF)
    which = lax.broadcasted_iota(jnp.int32, (J, EF), 0)
    sym_ij = jnp.full((J, EF), sym_ij_ref[first], jnp.int32)
    for j in range(1, J):
        sym_ij = jnp.where(which == j, sym_ij_ref[first + j], sym_ij)
    masked = jnp.where(sym_ij == sym_ef, amp_ref[...].astype(jnp.float32), 0.0)
    for p in range(R):
        slabs[p] = masked[:, p * ef:(p + 1) * ef]

    pl.semaphore_wait(barrier, R + C - 2)

    sends = []
    for d in range(1, R):
        to = lax.rem(r + d, R)
        send = remote(slabs.at[to], met.at[r], s1.at[d], r1.at[d], row=to)
        send.start()
        sends.append(send)
    met[r] = slabs[r]
    for send in sends:
        send.wait_recv()
    for p in range(R):
        rows16[pl.ds(p * J, J), :] = met[p]
    gathered[c] = rows16[...].astype(jnp.bfloat16)

    more = []
    for d in range(1, C):
        to = lax.rem(c + d, C)
        send = remote(gathered.at[c], gathered.at[c], s2.at[d], r2.at[d], col=to)
        send.start()
        more.append(send)

    total_rows = R * C * J
    group = next(g for g in (8, 4, 2, 1) if Q % min(g, Q) == 0 and min(g, Q) * C * J <= 256)
    group = min(group, Q)
    picks = []
    for half in range(2):
        for start in range(0, Q, group):
            blocks = []
            for p in range(start, start + group):
                at = lax.broadcasted_iota(jnp.int32, (C * J, total_rows), 0)
                source = (at // J) * (R * J) + (2 * p + half) * J + lax.rem(at, J)
                blocks.append(source == lax.broadcasted_iota(jnp.int32, (C * J, total_rows), 1))
            picks.append((half, start, blocks))

    for send in more:
        send.wait_recv()
    everything = gathered[...].reshape(total_rows, ef)
    for half, start, blocks in picks:
        pick = jnp.concatenate([jnp.where(b, 1.0, 0.0) for b in blocks], axis=0).astype(jnp.bfloat16)
        allowed[half, pl.ds(start * C * J, group * C * J), :] = jnp.dot(
            pick, everything, preferred_element_type=jnp.float32
        ).astype(jnp.bfloat16)

    cuts = chunks(ab, N)

    def multiply(half, j):
        at, size = cuts[j]
        part[j][half] = jnp.dot(allowed[half], panel_v[:, pl.ds(at, size)], preferred_element_type=jnp.float32)

    load.wait()
    pairs, chips, last = [], [], []

    def reduce_pair(j):
        pairs[j].wait_recv()
        for p in range(Q):
            at = pl.ds(p * C * J, C * J)
            summed[j][p] = part[j][k, at, :] + from_pair[j][at, :]
        chips.append([])
        for d in range(1, Q):
            to = lax.rem(q + d, Q)
            send = remote(summed[j].at[to], from_chips[j].at[d - 1], s4.at[j, d], r4.at[j, d], row=2 * to + k)
            send.start()
            chips[j].append(send)

    for j in range(len(cuts)):
        multiply(1 - k, j)
        pair = remote(part[j].at[1 - k], from_pair[j], s3.at[j], r3.at[j], row=2 * q + 1 - k)
        pair.start()
        pairs.append(pair)
        multiply(k, j)
        if j > 0:
            reduce_pair(j - 1)
    reduce_pair(len(cuts) - 1)

    for j in range(len(cuts)):
        total = summed[j][q]
        for d, send in enumerate(chips[j]):
            send.wait_recv()
            total = total + from_chips[j][d]
        for p in range(C):
            outgoing[j][p] = total[p * J:(p + 1) * J, :]
        last.append([])
        for d in range(1, C):
            to = lax.rem(c + d, C)
            send = remote(outgoing[j].at[to], landed[j].at[c], s5.at[j, d], r5.at[j, d], col=to)
            send.start()
            last[j].append(send)
        landed[j][c] = outgoing[j][c]
    for j, (at, size) in enumerate(cuts):
        for send in last[j]:
            send.wait_recv()
        for p in range(C):
            out_ref[:, p * ab + at:p * ab + at + size] = landed[j][p].astype(jnp.bfloat16)
    for send in sends + more + pairs + sum(chips, []) + sum(last, []):
        send.wait_send()


def solution(mesh):
    R, C = mesh.shape["row"], mesh.shape["col"]

    def body(amplitudes, panel, irrep_ij, irrep_ef):
        J, EF = amplitudes.shape
        ab, ef = panel.shape
        N = max(1, min(CHUNKS, ab // 512))
        widths = [size for _, size in chunks(ab, N)]
        Q = R // 2
        H = Q * C * J
        f32, bf16 = jnp.float32, jnp.bfloat16
        dma = pltpu.SemaphoreType.DMA
        if R * C <= 64 and J == 2 and ef <= 1024:
            exchange = direct
            buffers = [
                pltpu.VMEM((R, J * 8, 128), f32),
                pltpu.VMEM((R, J * 8, 128), bf16),
                pltpu.VMEM((pl.cdiv(ef, 128), 2, H, R * C * J * 8), f32),
                pltpu.VMEM((R * C, J * 8, 128), bf16),
            ]
            semaphores = [dma((R * C,)), dma((R * C,))]
        else:
            exchange = staged
            buffers = [
                pltpu.VMEM((R, J, ef), f32),
                pltpu.VMEM((R, J, ef), f32),
                pltpu.VMEM((R * J, ef), f32),
                pltpu.VMEM((C, R * J, ef), bf16),
            ]
            semaphores = [dma((R,)), dma((R,)), dma((C,)), dma((C,))]
        return pl.pallas_call(
            functools.partial(exchange, R, C, N),
            out_shape=jax.ShapeDtypeStruct((J, C * ab), bf16),
            in_specs=[
                pl.BlockSpec(memory_space=pltpu.VMEM),
                pl.BlockSpec(memory_space=pltpu.SMEM),
                pl.BlockSpec(memory_space=pltpu.VMEM),
                pl.BlockSpec(memory_space=pl.ANY),
            ],
            out_specs=pl.BlockSpec(memory_space=pltpu.VMEM),
            scratch_shapes=[
                pltpu.VMEM((ef, ab), bf16),
                *buffers,
                pltpu.VMEM((2, H, ef), bf16),
                [pltpu.VMEM((2, H, w), f32) for w in widths],
                [pltpu.VMEM((H, w), f32) for w in widths],
                [pltpu.VMEM((Q, C * J, w), f32) for w in widths],
                [pltpu.VMEM((max(Q - 1, 1), C * J, w), f32) for w in widths],
                [pltpu.VMEM((C, J, w), f32) for w in widths],
                [pltpu.VMEM((C, J, w), f32) for w in widths],
                dma,
                *semaphores,
                dma((N,)), dma((N,)),
                dma((N, Q)), dma((N, Q)),
                dma((N, C)), dma((N, C)),
            ],
            compiler_params=pltpu.CompilerParams(
                collective_id=0, has_side_effects=True, vmem_limit_bytes=60 << 20
            ),
            cost_estimate=pl.CostEstimate(
                flops=2 * R * C * J * ef * ab, bytes_accessed=2 * ab * ef, transcendentals=0
            ),
        )(amplitudes, irrep_ij, irrep_ef, panel.T)

    in_specs = (P(("col", "row"), None), P("col", "row"), P(), P())
    return jax.shard_map(body, mesh=mesh, in_specs=in_specs, out_specs=P(("col", "row"), None), check_vma=False)
```

```python
import functools

import jax
import jax.numpy as jnp
from jax import lax
from jax.experimental import pallas as pl
from jax.experimental.pallas import tpu as pltpu
from jax.sharding import PartitionSpec as P

CHUNKS = 3


def chunks(ab, n):
    step = ab // n // 128 * 128
    return [(j * step, step if j < n - 1 else ab - j * step) for j in range(n)]


def remote(src, dst, send_sem, recv_sem, **device):
    return pltpu.make_async_remote_copy(
        src_ref=src, dst_ref=dst, send_sem=send_sem, recv_sem=recv_sem,
        device_id=device, device_id_type=pl.DeviceIdType.MESH,
    )


def direct(R, C, N, amp_ref, sym_ij_ref, sym_ef_ref, panel_ref, out_ref,
           panel_v, wide, slabs, mate, both, pick, gathered, allowed, part, from_pair, summed, from_chips, outgoing, landed,
           panel_sem, s1, r1, s2, r2, s3, r3, s4, r4, s5, r5):
    r = lax.axis_index("row")
    c = lax.axis_index("col")
    k = lax.rem(r, 2)
    q = r // 2
    Q = R // 2
    J, EF = amp_ref.shape
    ef = EF // R
    ab = panel_v.shape[1]

    load = pltpu.make_async_copy(panel_ref, panel_v, panel_sem)
    load.start()

    lanes = [(at, min(128, ef - at)) for at in range(0, ef, 128)]
    L = 8
    peers = [(dq, m) for m in range(C) for dq in range(Q) if (dq, m) != (0, 0)]

    def partner(m):
        col, bit = c, 1
        while bit < C:
            if m & bit:
                col = col + bit - 2 * bit * lax.rem(c // bit, 2)
            bit *= 2
        return col

    barrier = pltpu.get_barrier_semaphore()
    for dq, m in peers:
        pl.semaphore_signal(
            barrier, inc=1, device_id={"row": 2 * lax.rem(q + dq, Q) + k, "col": partner(m)},
            device_id_type=pl.DeviceIdType.MESH,
        )
    pl.semaphore_signal(
        barrier, inc=1, device_id={"row": 2 * q + 1 - k}, device_id_type=pl.DeviceIdType.MESH
    )

    first = (c * R + r) * J
    sym_ef = sym_ef_ref[...].reshape(1, EF)
    which = lax.broadcasted_iota(jnp.int32, (J, EF), 0)
    sym_ij = jnp.full((J, EF), sym_ij_ref[first], jnp.int32)
    for j in range(1, J):
        sym_ij = jnp.where(which == j, sym_ij_ref[first + j], sym_ij)
    masked = jnp.where(sym_ij == sym_ef, amp_ref[...].astype(jnp.float32), 0.0)
    wide[...] = jnp.zeros_like(wide)
    for p in range(R):
        for i, (at, size) in enumerate(lanes):
            for j in range(J):
                wide[p, j * L + i:j * L + i + 1, 0:size] = masked[j:j + 1, p * ef + at:p * ef + at + size]
    for p in range(R):
        slabs[p % 2, p // 2] = wide[p].astype(jnp.bfloat16)

    pl.semaphore_wait(barrier, Q * C)

    swap = remote(slabs.at[1 - k], mate, s2, r2, row=2 * q + 1 - k)
    swap.start()
    for p in range(Q):
        both[p, k] = slabs[k, p]
    swap.wait_recv()
    for p in range(Q):
        both[p, 1 - k] = mate[p]

    sends = []
    for dq, m in peers:
        to = lax.rem(q + dq, Q)
        send = remote(both.at[to], gathered.at[c, q], s1.at[m, dq], r1.at[m, dq], row=2 * to + k, col=partner(m))
        send.start()
        sends.append((m, send))
    gathered[c, q] = both[q]
    held = lax.broadcasted_iota(jnp.int32, (J, R * J * L), 1)
    base = lax.broadcasted_iota(jnp.int32, (J, R * J * L), 0) * L
    for half in range(2):
        for p in range(Q):
            for i in range(len(lanes)):
                pick[i, pl.ds((half * Q + p) * J, J), :] = jnp.where(
                    base + ((2 * p + half) * J * L + i) == held, 1.0, 0.0)
    picks = pick[...].reshape(len(lanes) * R * J, R * J * L).astype(jnp.bfloat16)

    pairs, chips, last = [], [], []

    def finish_pair(m):
        pairs[m].wait_recv()
        both_cores = part[m, k] + from_pair[m]
        chips.append([])
        for p in range(Q):
            summed[m, p] = both_cores[p * J:(p + 1) * J, :]
        for d in range(1, Q):
            to = lax.rem(q + d, Q)
            send = remote(summed.at[m, to], from_chips.at[m, d - 1], s4.at[m, d], r4.at[m, d], row=2 * to + k)
            send.start()
            chips[m].append(send)

    def finish_chips(m):
        total = summed[m, q]
        for d, send in enumerate(chips[m]):
            send.wait_recv()
            total = total + from_chips[m, d]
        if m == 0:
            landed[c] = total
            return
        outgoing[m] = total
        send = remote(outgoing.at[m], landed.at[c], s5.at[m], r5.at[m], col=partner(m))
        send.start()
        last.append(send)

    for m in range(C):
        for n, send in sends:
            if n == m:
                send.wait_recv()
        block = gathered[partner(m)].reshape(R * J * L, 128)
        picked = jnp.dot(picks, block, preferred_element_type=jnp.float32)
        for i, (at, size) in enumerate(lanes):
            allowed[m, :, at:at + size] = picked[i * R * J:(i + 1) * R * J, :size].astype(jnp.bfloat16)
        if m == 0:
            load.wait()
        left = allowed[m]
        for at, size in chunks(ab, N):
            product = jnp.dot(left, panel_v[:, pl.ds(at, size)], preferred_element_type=jnp.float32)
            part[m, 0, :, pl.ds(at, size)] = product[:Q * J]
            part[m, 1, :, pl.ds(at, size)] = product[Q * J:]
        pair = remote(part.at[m, 1 - k], from_pair.at[m], s3.at[m], r3.at[m], row=2 * q + 1 - k)
        pair.start()
        pairs.append(pair)
        if m > 0:
            finish_pair(m - 1)
    finish_pair(C - 1)
    for m in range(C):
        finish_chips(m)
    for send in last:
        send.wait_recv()
    for p in range(C):
        out_ref[:, p * ab:(p + 1) * ab] = landed[p].astype(jnp.bfloat16)
    for send in [send for _, send in sends] + [swap] + pairs + sum(chips, []) + last:
        send.wait_send()


def staged(R, C, N, amp_ref, sym_ij_ref, sym_ef_ref, panel_ref, out_ref,
           panel_v, slabs, met, rows16, gathered, allowed, part, from_pair, summed, from_chips, outgoing, landed,
           panel_sem, s1, r1, s2, r2, s3, r3, s4, r4, s5, r5):
    r = lax.axis_index("row")
    c = lax.axis_index("col")
    k = lax.rem(r, 2)
    q = r // 2
    Q = R // 2
    J, EF = amp_ref.shape
    ef = EF // R
    ab = panel_v.shape[1]

    load = pltpu.make_async_copy(panel_ref, panel_v, panel_sem)
    load.start()

    barrier = pltpu.get_barrier_semaphore()
    for d in range(1, R):
        pl.semaphore_signal(barrier, inc=1, device_id={"row": lax.rem(r + d, R)}, device_id_type=pl.DeviceIdType.MESH)
    for d in range(1, C):
        pl.semaphore_signal(barrier, inc=1, device_id={"col": lax.rem(c + d, C)}, device_id_type=pl.DeviceIdType.MESH)

    first = (c * R + r) * J
    sym_ef = sym_ef_ref[...].reshape(1, EF)
    which = lax.broadcasted_iota(jnp.int32, (J, EF), 0)
    sym_ij = jnp.full((J, EF), sym_ij_ref[first], jnp.int32)
    for j in range(1, J):
        sym_ij = jnp.where(which == j, sym_ij_ref[first + j], sym_ij)
    masked = jnp.where(sym_ij == sym_ef, amp_ref[...].astype(jnp.float32), 0.0)
    for p in range(R):
        slabs[p] = masked[:, p * ef:(p + 1) * ef]

    pl.semaphore_wait(barrier, R + C - 2)

    sends = []
    for d in range(1, R):
        to = lax.rem(r + d, R)
        send = remote(slabs.at[to], met.at[r], s1.at[d], r1.at[d], row=to)
        send.start()
        sends.append(send)
    met[r] = slabs[r]
    for send in sends:
        send.wait_recv()
    for p in range(R):
        rows16[pl.ds(p * J, J), :] = met[p]
    gathered[c] = rows16[...].astype(jnp.bfloat16)

    more = []
    for d in range(1, C):
        to = lax.rem(c + d, C)
        send = remote(gathered.at[c], gathered.at[c], s2.at[d], r2.at[d], col=to)
        send.start()
        more.append(send)

    total_rows = R * C * J
    group = next(g for g in (8, 4, 2, 1) if Q % min(g, Q) == 0 and min(g, Q) * C * J <= 256)
    group = min(group, Q)
    picks = []
    for half in range(2):
        for start in range(0, Q, group):
            blocks = []
            for p in range(start, start + group):
                at = lax.broadcasted_iota(jnp.int32, (C * J, total_rows), 0)
                source = (at // J) * (R * J) + (2 * p + half) * J + lax.rem(at, J)
                blocks.append(source == lax.broadcasted_iota(jnp.int32, (C * J, total_rows), 1))
            picks.append((half, start, blocks))

    for send in more:
        send.wait_recv()
    everything = gathered[...].reshape(total_rows, ef)
    for half, start, blocks in picks:
        pick = jnp.concatenate([jnp.where(b, 1.0, 0.0) for b in blocks], axis=0).astype(jnp.bfloat16)
        allowed[half, pl.ds(start * C * J, group * C * J), :] = jnp.dot(
            pick, everything, preferred_element_type=jnp.float32
        ).astype(jnp.bfloat16)

    cuts = chunks(ab, N)

    def multiply(half, j):
        at, size = cuts[j]
        part[j][half] = jnp.dot(allowed[half], panel_v[:, pl.ds(at, size)], preferred_element_type=jnp.float32)

    load.wait()
    pairs, chips, last = [], [], []

    def reduce_pair(j):
        pairs[j].wait_recv()
        for p in range(Q):
            at = pl.ds(p * C * J, C * J)
            summed[j][p] = part[j][k, at, :] + from_pair[j][at, :]
        chips.append([])
        for d in range(1, Q):
            to = lax.rem(q + d, Q)
            send = remote(summed[j].at[to], from_chips[j].at[d - 1], s4.at[j, d], r4.at[j, d], row=2 * to + k)
            send.start()
            chips[j].append(send)

    for j in range(len(cuts)):
        multiply(1 - k, j)
        pair = remote(part[j].at[1 - k], from_pair[j], s3.at[j], r3.at[j], row=2 * q + 1 - k)
        pair.start()
        pairs.append(pair)
        multiply(k, j)
        if j > 0:
            reduce_pair(j - 1)
    reduce_pair(len(cuts) - 1)

    for j in range(len(cuts)):
        total = summed[j][q]
        for d, send in enumerate(chips[j]):
            send.wait_recv()
            total = total + from_chips[j][d]
        for p in range(C):
            outgoing[j][p] = total[p * J:(p + 1) * J, :]
        last.append([])
        for d in range(1, C):
            to = lax.rem(c + d, C)
            send = remote(outgoing[j].at[to], landed[j].at[c], s5.at[j, d], r5.at[j, d], col=to)
            send.start()
            last[j].append(send)
        landed[j][c] = outgoing[j][c]
    for j, (at, size) in enumerate(cuts):
        for send in last[j]:
            send.wait_recv()
        for p in range(C):
            out_ref[:, p * ab + at:p * ab + at + size] = landed[j][p].astype(jnp.bfloat16)
    for send in sends + more + pairs + sum(chips, []) + sum(last, []):
        send.wait_send()


def solution(mesh):
    R, C = mesh.shape["row"], mesh.shape["col"]

    def body(amplitudes, panel, irrep_ij, irrep_ef):
        J, EF = amplitudes.shape
        ab, ef = panel.shape
        N = max(1, min(CHUNKS, ab // 512))
        widths = [size for _, size in chunks(ab, N)]
        Q = R // 2
        H = Q * C * J
        f32, bf16 = jnp.float32, jnp.bfloat16
        dma = pltpu.SemaphoreType.DMA
        if C & (C - 1) == 0 and 2 <= Q <= 4 and J == 2 and ef <= 1024:
            exchange = direct
            buffers = [
                pltpu.VMEM((R, J * 8, 128), f32),
                pltpu.VMEM((2, Q, J * 8, 128), bf16),
                pltpu.VMEM((Q, J * 8, 128), bf16),
                pltpu.VMEM((Q, 2, J * 8, 128), bf16),
                pltpu.VMEM((pl.cdiv(ef, 128), R * J, R * J * 8), f32),
                pltpu.VMEM((C, Q, 2, J * 8, 128), bf16),
                pltpu.VMEM((C, R * J, ef), bf16),
                pltpu.VMEM((C, 2, Q * J, ab), f32),
                pltpu.VMEM((C, Q * J, ab), f32),
                pltpu.VMEM((C, Q, J, ab), f32),
                pltpu.VMEM((C, Q - 1, J, ab), f32),
                pltpu.VMEM((C, J, ab), f32),
                pltpu.VMEM((C, J, ab), f32),
            ]
            semaphores = [dma((C, Q)), dma((C, Q)), dma, dma, dma((C,)), dma((C,)), dma((C, Q)), dma((C, Q)), dma((C,)), dma((C,))]
        else:
            exchange = staged
            buffers = [
                pltpu.VMEM((R, J, ef), f32),
                pltpu.VMEM((R, J, ef), f32),
                pltpu.VMEM((R * J, ef), f32),
                pltpu.VMEM((C, R * J, ef), bf16),
                pltpu.VMEM((2, H, ef), bf16),
                [pltpu.VMEM((2, H, w), f32) for w in widths],
                [pltpu.VMEM((H, w), f32) for w in widths],
                [pltpu.VMEM((Q, C * J, w), f32) for w in widths],
                [pltpu.VMEM((max(Q - 1, 1), C * J, w), f32) for w in widths],
                [pltpu.VMEM((C, J, w), f32) for w in widths],
                [pltpu.VMEM((C, J, w), f32) for w in widths],
            ]
            semaphores = [
                dma((R,)), dma((R,)), dma((C,)), dma((C,)),
                dma((N,)), dma((N,)),
                dma((N, Q)), dma((N, Q)),
                dma((N, C)), dma((N, C)),
            ]
        return pl.pallas_call(
            functools.partial(exchange, R, C, N),
            out_shape=jax.ShapeDtypeStruct((J, C * ab), bf16),
            in_specs=[
                pl.BlockSpec(memory_space=pltpu.VMEM),
                pl.BlockSpec(memory_space=pltpu.SMEM),
                pl.BlockSpec(memory_space=pltpu.VMEM),
                pl.BlockSpec(memory_space=pl.ANY),
            ],
            out_specs=pl.BlockSpec(memory_space=pltpu.VMEM),
            scratch_shapes=[
                pltpu.VMEM((ef, ab), bf16),
                *buffers,
                dma,
                *semaphores,
            ],
            compiler_params=pltpu.CompilerParams(
                collective_id=0, has_side_effects=True, vmem_limit_bytes=60 << 20
            ),
            cost_estimate=pl.CostEstimate(
                flops=2 * R * C * J * ef * ab, bytes_accessed=2 * ab * ef, transcendentals=0
            ),
        )(amplitudes, irrep_ij, irrep_ef, panel.T)

    in_specs = (P(("col", "row"), None), P("col", "row"), P(), P())
    return jax.shard_map(body, mesh=mesh, in_specs=in_specs, out_specs=P(("col", "row"), None), check_vma=False)
```
